768 devices in a mesh: dp: 96 (over y, x, z_lo), node: 8 (over z_hi, core).
Axes of the slice: x: 4, y: 8, z: 12 (z_hi: 4, z_lo: 3; z = z_hi * 3 + z_lo), core: 2. Of those that a mesh axis runs over, the one named last changes fastest.
Arguments:
- acts: bfloat16 [98304, 8192], P(('dp', 'node')), may hold values from -6 to 6
- cotangent: bfloat16 [98304, 512], P(('dp', 'node')), may hold values from -6 to 6
- w_values: bfloat16 [8192, 512], P('node'), may hold values from -0.25 to 0.25
- w_scales: float32 [64], P('node'), may hold values from 0.5 to 4
Outputs:
- input_grad: bfloat16 [98304, 8192], P('dp', 'node')
- weight_grad: float32 [8192, 512], P('node')
The draws below stay inside these ranges and needn't reach their ends.
All inputs are finite; a program needn't handle non-finite values. Where the reference program divides by a largest or mean magnitude, that divisor is 1e-20 or more.
Results may differ from the reference program's by a relative error of at most 0.012.
Values may be sent and summed in bfloat16 or wider, within the bound.
No kernel may reach another device: no remote copies, remote signals or barrier semaphores. Data moves between devices by JAX's collectives and lax.ppermute only.
A program may use at most 32 MiB of HBM per device.

```python
import math
import jax
import jax.numpy as jnp
from jax import lax

D = 8192
HD = 512
TOK_DEV = 128
TOKENS = 98304
N_DP = 96
N_NODE = 8


def shard_levels(rng, shape, pieces, low, top_value):
    def one(position, blocks):
        heights = jax.random.uniform(jax.random.fold_in(jax.random.fold_in(rng, 6), position), (blocks,), jnp.float32, low / len(pieces), top_value / len(pieces))
        return jnp.repeat(jnp.exp(heights), shape[position] // blocks).reshape((-1,) + (1,) * (len(shape) - position - 1))

    level = one(*pieces[0])
    for cut in pieces[1:]:
        level = level * one(*cut)
    return level


def scatter_about(own_key, shape, scale, limit, shards=(), held_as=jnp.bfloat16):
    values = scale * jax.random.normal(own_key, shape, jnp.float32)
    if shards:
        values = values * shard_levels(own_key, shape, shards, -0.22, 0.18)
    return jnp.clip(values, -limit, limit).astype(held_as)


def setup_inputs(seed: int = 0) -> dict:
    key_of = jax.random.split(jax.random.key(seed), 5)
    acts = scatter_about(key_of[0], (TOKENS, D), 1.0, 6.0, ((0, 768),))
    cotangent = scatter_about(key_of[1], (TOKENS, HD), 1.0, 6.0, ((0, 768),))
    w_values = scatter_about(key_of[2], (D, HD), HD ** -0.5, 0.25, ((0, 8),))
    w_scales = jnp.clip(jnp.exp(math.log(4.0) - 2.0794415 * jax.random.uniform(key_of[3], (D // 128,), jnp.float32) ** shard_levels(key_of[3], (D // 128,), ((0, 8),), -0.2, 0.2)), 0.5, 4.0)
    return {"acts": acts, "cotangent": cotangent, "w_values": w_values, "w_scales": w_scales}


def block_quant(grad):
    scale = jnp.max(jnp.abs(grad), axis=(-2, -1), keepdims=True) + 1e-6
    values = (grad / scale).astype(jnp.bfloat16)
    return values, scale


def reference(acts, cotangent, w_values, w_scales):
    nblocks = D // 128
    weight = (w_values.astype(jnp.float32).reshape(nblocks, 128, HD) * w_scales[:, None, None]).reshape(D, HD).astype(jnp.bfloat16)
    input_grad = lax.dot_general(cotangent, weight, (((1,), (1,)), ((), ())), preferred_element_type=jnp.float32).astype(jnp.bfloat16)
    groups_x = acts.reshape(N_DP, N_NODE, TOK_DEV, D)
    groups_y = cotangent.reshape(N_DP, N_NODE, TOK_DEV, HD)

    def one_group(total, pair):
        block_x, block_y = pair
        partial_value = jnp.einsum("ptd,pte->pde", block_x.astype(jnp.float32), block_y.astype(jnp.float32))
        values, scale = block_quant(partial_value.reshape(N_NODE, nblocks, 128, HD))
        node_sum = jnp.sum(values.astype(jnp.float32) * scale, axis=0)
        rvalues, rscale = block_quant(node_sum)
        return total + rvalues.astype(jnp.float32) * rscale, None

    start = jnp.zeros((nblocks, 128, HD), jnp.float32)
    total, unused = lax.scan(one_group, start, (groups_x, groups_y))
    weight_grad = total.reshape(D, HD) * (TOKENS ** -0.5)
    return input_grad, weight_grad
```

```python
import jax
import jax.numpy as jnp
from jax import lax
from jax.sharding import Mesh
from jax.sharding import PartitionSpec as P

AXES = ("y", "x", "zl", "zh", "c")
SIZES = (8, 4, 3, 4, 2)


def input_gradient(peers, w_values, w_scales):
    head = w_values.shape[1]
    blocks = w_values.shape[0] // 128
    weight = (
        (w_values.astype(jnp.float32).reshape(blocks, 128, head) * w_scales[:, None, None])
        .reshape(blocks * 128, head)
        .astype(jnp.bfloat16)
    )
    columns = lax.dot_general(
        peers, weight, (((1,), (1,)), ((), ())), preferred_element_type=jnp.float32
    )
    return columns.astype(jnp.bfloat16)


def exchange(value, axes):
    return lax.all_to_all(value, axes, split_axis=0, concat_axis=0, tiled=True)


def spread(value, axes, size):
    copies = lax.optimization_barrier(jnp.broadcast_to(value[None], (size,) + value.shape))
    return exchange(copies, axes)


def weight_gradient(acts, cotangent, factor):
    tok, width = acts.shape
    head = cotangent.shape[1]
    ny, nx, nzl, nzh, nc = SIZES
    owned = width // (nzh * nc)
    part = owned // nx
    rows = part // ny
    by_x = jnp.moveaxis(acts.reshape(tok, nzh * nc, nx, part), 2, 0).reshape(nx, tok, nzh * nc * part)
    both = jnp.concatenate([by_x, jnp.broadcast_to(cotangent[None], (nx, tok, head))], axis=2)
    got = exchange(both, "x").reshape(nx * tok, nzh * nc * part + head)
    partial = lax.dot_general(
        got[:, : nzh * nc * part],
        got[:, nzh * nc * part :],
        (((0,), (0,)), ((), ())),
        preferred_element_type=jnp.float32,
    )
    partial = partial.reshape(nzh, nc, ny, rows, head).transpose(1, 2, 0, 3, 4)
    over_c = exchange(partial.astype(jnp.bfloat16), "c")
    chip = jnp.sum(over_c.astype(jnp.float32), axis=0).astype(jnp.bfloat16)
    over_y = jnp.sum(exchange(chip, "y").astype(jnp.float32), axis=0).astype(jnp.bfloat16)
    half = rows // 2
    slots = over_y.reshape(nzh, 2, half, head)
    slots = jnp.concatenate([slots, jnp.zeros((nzh, 1, half, head), jnp.bfloat16)], axis=1)
    slots = slots.reshape(nzh * nzl, half, head)
    total = jnp.sum(exchange(slots, ("zh", "zl")).astype(jnp.float32), axis=0).astype(jnp.bfloat16)
    back = spread(total, ("y", "zl"), ny * nzl).reshape(ny, nzl, half, head)
    back = back[:, :2].reshape(part, head)
    full = spread(back, "x", nx).reshape(owned, head)
    return full.astype(jnp.float32) * factor


def local(acts, cotangent, w_values, w_scales):
    tokens = acts.shape[0] * 768
    peers = lax.all_gather(cotangent, ("zh", "c"), axis=0, tiled=True)
    input_grad = input_gradient(peers, w_values, w_scales)
    weight_grad = weight_gradient(acts, cotangent, tokens ** (-0.5))
    return (input_grad, weight_grad)


def solution(mesh):
    fine = Mesh(mesh.devices.reshape(SIZES), AXES)
    dp, node = ("y", "x", "zl"), ("zh", "c")
    placed = (P(dp + node, None), P(dp + node, None), P(node, None), P(node))
    return jax.shard_map(
        local,
        mesh=fine,
        in_specs=placed,
        out_specs=(P(dp, node), P(node, None)),
        check_vma=False,
    )
```

```python
import jax
import jax.numpy as jnp
from jax import lax
from jax.experimental import pallas as pl
from jax.experimental.pallas import tpu as pltpu
from jax.sharding import Mesh
from jax.sharding import PartitionSpec as P

AXES = ("y", "x", "zl", "zh", "c")
NY, NX, NZL, NZH, NC = SIZES = (8, 4, 3, 4, 2)
NODE = NZH * NC
SMALL = pltpu.CompilerParams(vmem_limit_bytes=12 * 2**20)


def exchange(value, axes):
    return lax.all_to_all(value, axes, split_axis=0, concat_axis=0, tiled=True)


def spread(value, axes, size):
    copies = lax.optimization_barrier(jnp.broadcast_to(value[None], (size,) + value.shape))
    return exchange(copies, axes)


def lay_out(acts, cotangent):
    tok, width = acts.shape
    head = cotangent.shape[1]
    part = width // (NODE * NX)
    step = 32

    def kernel(acts_ref, cot_ref, out_ref):
        for x in range(NX):
            for n in range(NODE):
                out_ref[x, :, n * part : (n + 1) * part] = acts_ref[:, pl.ds((n * NX + x) * part, part)]
            out_ref[x, :, NODE * part :] = cot_ref[...]

    return pl.pallas_call(
        kernel,
        grid=(tok // step,),
        in_specs=[
            pl.BlockSpec((step, width), lambda i: (i, 0)),
            pl.BlockSpec((step, head), lambda i: (i, 0)),
        ],
        out_specs=pl.BlockSpec((NX, step, NODE * part + head), lambda i: (0, i, 0)),
        out_shape=jax.ShapeDtypeStruct((NX, tok, NODE * part + head), jnp.bfloat16),
        compiler_params=SMALL,
        cost_estimate=pl.CostEstimate(flops=0, bytes_accessed=2 * NX * tok * (NODE * part + head) * 2, transcendentals=0),
    )(acts, cotangent)


def product(got, head, after):
    tokens, width = got.shape
    part = (width - head) // NODE
    rows = part // NY

    def kernel(acts_ref, cot_ref, *refs):
        out_ref = refs[-1]
        value = lax.dot_general(
            acts_ref[...], cot_ref[...], (((0,), (0,)), ((), ())), preferred_element_type=jnp.float32
        )
        out_ref[0, :, 0] = value.astype(jnp.bfloat16).reshape(NY, rows, head)

    return pl.pallas_call(
        kernel,
        grid=(NODE,),
        in_specs=[
            pl.BlockSpec((tokens, part), lambda n: (0, n)),
            pl.BlockSpec((tokens, head), lambda n: (0, NODE * part // head)),
        ]
        + [pl.BlockSpec(memory_space=pl.ANY)] * len(after),
        out_specs=pl.BlockSpec((1, NY, 1, rows, head), lambda n: (n % NC, 0, n // NC, 0, 0)),
        out_shape=jax.ShapeDtypeStruct((NC, NY, NZH, rows, head), jnp.bfloat16),
        compiler_params=SMALL,
        cost_estimate=pl.CostEstimate(
            flops=2 * tokens * NODE * part * head,
            bytes_accessed=(tokens * width + NODE * part * head) * 2,
            transcendentals=0,
        ),
    )(got, got, *after)


def add(value):
    return jnp.sum(value.astype(jnp.float32), axis=0).astype(jnp.bfloat16)


def add_copies(value, copies, axis, after=()):
    shape = value.shape[1:]
    out = shape[:axis] + (copies,) + shape[axis:]

    def kernel(value_ref, *refs):
        total = value_ref[0].astype(jnp.float32)
        for i in range(1, value.shape[0]):
            total = total + value_ref[i].astype(jnp.float32)
        total = total.astype(jnp.bfloat16)
        for i in range(copies):
            refs[-1][(slice(None),) * axis + (i,)] = total

    return pl.pallas_call(
        kernel,
        in_specs=[pl.BlockSpec(memory_space=pltpu.VMEM)] + [pl.BlockSpec(memory_space=pl.ANY)] * len(after),
        out_specs=pl.BlockSpec(memory_space=pltpu.VMEM),
        out_shape=jax.ShapeDtypeStruct(out, jnp.bfloat16),
        compiler_params=SMALL,
        cost_estimate=pl.CostEstimate(flops=value.size, bytes_accessed=value.size * 2, transcendentals=0),
    )(value, *after)


def input_gradient(peers, w_values, w_scales):
    head = w_values.shape[1]
    blocks = w_values.shape[0] // 128
    weight = (
        (w_values.astype(jnp.float32).reshape(blocks, 128, head) * w_scales[:, None, None])
        .reshape(blocks * 128, head)
        .astype(jnp.bfloat16)
    )
    columns = lax.dot_general(
        peers, weight, (((1,), (1,)), ((), ())), preferred_element_type=jnp.float32
    )
    return columns.astype(jnp.bfloat16)


def gather_zh(cotangent):
    return [cotangent] + [
        lax.ppermute(cotangent, "zh", [(i, (i + k) % NZH) for i in range(NZH)]) for k in range(1, NZH)
    ]


def gather_node(mine):
    here = lax.axis_index("zh")
    stack = jnp.stack(mine)
    ordered = jnp.concatenate(
        [lax.dynamic_slice_in_dim(stack, (here - j) % NZH, 1, 0) for j in range(NZH)], axis=0
    )
    other = lax.ppermute(ordered, "c", [(0, 1), (1, 0)])
    first = lax.axis_index("c") == 0
    return jnp.stack([jnp.where(first, ordered, other), jnp.where(first, other, ordered)], axis=1)


def local(acts, cotangent, w_values, w_scales):
    tok, width = acts.shape
    head = cotangent.shape[1]
    owned = width // NODE
    part = owned // NX
    rows = part // NY
    factor = (tok * NY * NX * NZL * NZH * NC) ** (-0.5)

    got = exchange(lay_out(acts, cotangent), "x")
    mine = gather_zh(cotangent)
    partial = product(got.reshape(NX * tok, NODE * part + head), head, mine[1:])
    chip = add(exchange(partial, "c"))

    over_y = exchange(chip, "y")
    peers = gather_node(mine).reshape(NODE * tok, head)
    input_grad = input_gradient(peers, w_values, w_scales)

    slots = add_copies(over_y, NZL, 1, [input_grad]).reshape(NZH * NZL, rows, head)
    total = add_copies(exchange(slots, ("zh", "zl")), NY, 0)
    back = exchange(total, "y").reshape(part, head)
    full = spread(back, "x", NX).reshape(owned, head)
    return (input_grad, full.astype(jnp.float32) * factor)


def solution(mesh):
    fine = Mesh(mesh.devices.reshape(SIZES), AXES)
    dp, node = ("y", "x", "zl"), ("zh", "c")
    placed = (P(dp + node, None), P(dp + node, None), P(node, None), P(node))
    return jax.shard_map(
        local,
        mesh=fine,
        in_specs=placed,
        out_specs=(P(dp, node), P(node, None)),
        check_vma=False,
    )
```

```python
import jax
import jax.numpy as jnp
from jax import lax
from jax.experimental import pallas as pl
from jax.experimental.pallas import tpu as pltpu
from jax.sharding import Mesh
from jax.sharding import PartitionSpec as P

AXES = ("y", "x", "zl", "zh", "c")
NY, NX, NZL, NZH, NC = SIZES = (8, 4, 3, 4, 2)
NODE = NZH * NC
SMALL = pltpu.CompilerParams(vmem_limit_bytes=12 * 2**20)


def exchange(value, axes):
    return lax.all_to_all(value, axes, split_axis=0, concat_axis=0, tiled=True)


def lay_out(acts, cotangent):
    tok, width = acts.shape
    head = cotangent.shape[1]
    part = width // (NODE * NX)
    step = 32

    def kernel(acts_ref, cot_ref, out_ref):
        for x in range(NX):
            for n in range(NODE):
                out_ref[x, :, n * part : (n + 1) * part] = acts_ref[:, pl.ds((n * NX + x) * part, part)]
            out_ref[x, :, NODE * part :] = cot_ref[...]

    return pl.pallas_call(
        kernel,
        grid=(tok // step,),
        in_specs=[
            pl.BlockSpec((step, width), lambda i: (i, 0)),
            pl.BlockSpec((step, head), lambda i: (i, 0)),
        ],
        out_specs=pl.BlockSpec((NX, step, NODE * part + head), lambda i: (0, i, 0)),
        out_shape=pltpu.HBM((NX, tok, NODE * part + head), jnp.bfloat16),
        compiler_params=SMALL,
        cost_estimate=pl.CostEstimate(flops=0, bytes_accessed=2 * NX * tok * (NODE * part + head) * 2, transcendentals=0),
    )(acts, cotangent)


def product(got, head, core, received=None, after=()):
    tokens, width = got.shape
    part = (width - head) // NODE
    rows = part // NY
    out = (NY, NZH, rows, head)
    block = pl.BlockSpec((NY, 1, rows, head), lambda n, core_ref: (0, n, 0, 0))
    more = [] if received is None else [received]

    def kernel(core_ref, acts_ref, cot_ref, *refs):
        value = lax.dot_general(
            acts_ref[...], cot_ref[...], (((0,), (0,)), ((), ())), preferred_element_type=jnp.float32
        ).reshape(NY, rows, head)
        if more:
            value = value + refs[0][:, 0].astype(jnp.float32)
        refs[-1][:, 0] = value.astype(jnp.bfloat16)

    return pl.pallas_call(
        kernel,
        grid_spec=pltpu.PrefetchScalarGridSpec(
            num_scalar_prefetch=1,
            grid=(NZH,),
            in_specs=[
                pl.BlockSpec((tokens, part), lambda n, core_ref: (0, n * NC + core_ref[0])),
                pl.BlockSpec((tokens, head), lambda n, core_ref: (0, NODE * part // head)),
            ]
            + [block] * len(more)
            + [pl.BlockSpec(memory_space=pl.ANY)] * len(after),
            out_specs=block,
        ),
        out_shape=pltpu.HBM(out, jnp.bfloat16) if more else jax.ShapeDtypeStruct(out, jnp.bfloat16),
        compiler_params=SMALL,
        cost_estimate=pl.CostEstimate(
            flops=tokens * NODE * part * head,
            bytes_accessed=tokens * width * 2,
            transcendentals=0,
        ),
    )(core, got, got, *more, *after)


def small_kernel(kernel, out, value, after=()):
    return pl.pallas_call(
        kernel,
        in_specs=[pl.BlockSpec(memory_space=pltpu.VMEM)] + [pl.BlockSpec(memory_space=pl.ANY)] * len(after),
        out_specs=pl.BlockSpec(memory_space=pltpu.VMEM),
        out_shape=jax.ShapeDtypeStruct(out, jnp.bfloat16),
        compiler_params=SMALL,
        cost_estimate=pl.CostEstimate(flops=value.size, bytes_accessed=value.size * 2, transcendentals=0),
    )(value, *after)


def total_of(ref, index):
    total = ref[(0,) + index].astype(jnp.float32)
    for i in range(1, ref.shape[0]):
        total = total + ref[(i,) + index].astype(jnp.float32)
    return total.astype(jnp.bfloat16)


PIECE, LANES = 16, 128


def pieces(rows, head):
    whole = (rows // PIECE) * (head // LANES)
    each = -(-whole // NZL)
    return each, [
        (p // each, p % each * PIECE, p % (rows // PIECE) * PIECE, p // (rows // PIECE) * LANES) for p in range(whole)
    ]


def sum_y(value, after):
    ny, nzh, rows, head = value.shape
    each, where = pieces(rows, head)

    def kernel(value_ref, *refs):
        out_ref = refs[-1]
        for zh in range(nzh):
            out_ref[zh, NZL - 1] = jnp.zeros(out_ref.shape[2:], jnp.bfloat16)
            for zl, slot, row, column in where:
                out_ref[zh, zl, slot : slot + PIECE] = total_of(
                    value_ref, (zh, slice(row, row + PIECE), slice(column, column + LANES))
                )

    return small_kernel(kernel, (nzh, NZL, each * PIECE, LANES), value, after)


def sum_z(value):
    def kernel(value_ref, out_ref):
        total = total_of(value_ref, ())
        for i in range(NY * NZL):
            out_ref[i] = total

    return small_kernel(kernel, (NY * NZL,) + value.shape[1:], value)


def join(value, rows, head):
    _, where = pieces(rows, head)

    def kernel(value_ref, out_ref):
        for y in range(NY):
            for zl, slot, row, column in where:
                piece = value_ref[y, zl, slot : slot + PIECE]
                for x in range(NX):
                    out_ref[x, y, row : row + PIECE, column : column + LANES] = piece

    return small_kernel(kernel, (NX, NY, rows, head), value)


def input_gradient(peers, w_values, w_scales):
    head = w_values.shape[1]
    blocks = w_values.shape[0] // 128
    weight = (
        (w_values.astype(jnp.float32).reshape(blocks, 128, head) * w_scales[:, None, None])
        .reshape(blocks * 128, head)
        .astype(jnp.bfloat16)
    )
    columns = lax.dot_general(
        peers, weight, (((1,), (1,)), ((), ())), preferred_element_type=jnp.float32
    )
    return columns.astype(jnp.bfloat16)


def gather_zh(cotangent):
    return [cotangent] + [
        lax.ppermute(cotangent, "zh", [(i, (i + k) % NZH) for i in range(NZH)]) for k in range(1, NZH)
    ]


def gather_node(mine):
    here = lax.axis_index("zh")
    stack = jnp.stack(mine)
    ordered = jnp.concatenate(
        [lax.dynamic_slice_in_dim(stack, (here - j) % NZH, 1, 0) for j in range(NZH)], axis=0
    )
    other = lax.ppermute(ordered, "c", [(0, 1), (1, 0)])
    first = lax.axis_index("c") == 0
    return jnp.stack([jnp.where(first, ordered, other), jnp.where(first, other, ordered)], axis=1)


def local(acts, cotangent, w_values, w_scales):
    tok, width = acts.shape
    head = cotangent.shape[1]
    owned = width // NODE
    part = owned // NX
    rows = part // NY
    factor = (tok * NY * NX * NZL * NZH * NC) ** (-0.5)

    core = lax.axis_index("c")[None]
    got = exchange(lay_out(acts, cotangent), "x").reshape(NX * tok, NODE * part + head)
    mine = gather_zh(cotangent)
    theirs = product(got, head, 1 - core, after=mine[1:])
    chip = product(got, head, core, received=lax.ppermute(theirs, "c", [(0, 1), (1, 0)]))

    over_y = exchange(chip, "y")
    peers = gather_node(mine).reshape(NODE * tok, head)
    input_grad = input_gradient(peers, w_values, w_scales)

    slots = sum_y(over_y, [input_grad])
    slots = slots.reshape((NZH * NZL,) + slots.shape[2:])
    copies = sum_z(exchange(slots, ("zh", "zl")))
    back = exchange(copies, ("y", "zl"))
    back = join(back.reshape((NY, NZL) + back.shape[1:]), rows, head)
    full = exchange(back, "x").reshape(owned, head)
    return (input_grad, full.astype(jnp.float32) * factor)


def solution(mesh):
    fine = Mesh(mesh.devices.reshape(SIZES), AXES)
    dp, node = ("y", "x", "zl"), ("zh", "c")
    placed = (P(dp + node, None), P(dp + node, None), P(node, None), P(node))
    return jax.shard_map(
        local,
        mesh=fine,
        in_specs=placed,
        out_specs=(P(dp, node), P(node, None)),
        check_vma=False,
    )
```

```python
import jax
import jax.numpy as jnp
from jax import lax
from jax.experimental import pallas as pl
from jax.experimental.pallas import tpu as pltpu
from jax.sharding import Mesh
from jax.sharding import PartitionSpec as P

AXES = ("yh", "yl", "x", "zl", "zh", "c")
NYH, NYL, NX, NZL, NZH, NC = SIZES = (4, 2, 4, 3, 4, 2)
NODE = NZH * NC
NEAR = NX * NYL
LARGE = pltpu.CompilerParams(vmem_limit_bytes=60 * 2**20)
SMALL = pltpu.CompilerParams(vmem_limit_bytes=12 * 2**20)


def exchange(value, axes):
    return lax.all_to_all(value, axes, split_axis=0, concat_axis=0, tiled=True)


def lay_out(acts, cotangent):
    tok, width = acts.shape
    head = cotangent.shape[1]
    part = width // (NODE * NEAR)
    step = 32

    def kernel(acts_ref, cot_ref, out_ref):
        for s in range(NEAR):
            for c in range(NC):
                for zh in range(NZH):
                    to, source = (c * NZH + zh) * part, ((zh * NC + c) * NEAR + s) * part
                    out_ref[s, :, to : to + part] = acts_ref[:, source : source + part]
            out_ref[s, :, NODE * part :] = cot_ref[...]

    out = (NEAR, tok, NODE * part + head)
    return pl.pallas_call(
        kernel,
        grid=(tok // step,),
        in_specs=[
            pl.BlockSpec((step, width), lambda i: (i, 0)),
            pl.BlockSpec((step, head), lambda i: (i, 0)),
        ],
        out_specs=pl.BlockSpec((NEAR, step, out[2]), lambda i: (0, i, 0)),
        out_shape=pltpu.HBM(out, jnp.bfloat16),
        compiler_params=LARGE,
        cost_estimate=pl.CostEstimate(flops=0, bytes_accessed=4 * NEAR * tok * out[2], transcendentals=0),
    )(acts, cotangent)


def product(got, head, core, received=None, after=()):
    tokens, width = got.shape
    part = (width - head) // NODE
    rows = part // NYH
    group = 2
    out = (NYH, NZH, rows, head)
    block = pl.BlockSpec((NYH, group, rows, head), lambda n, core_ref: (0, n, 0, 0))
    more = [] if received is None else [received]

    def kernel(core_ref, acts_ref, cot_ref, *refs):
        value = lax.dot_general(
            acts_ref[...], cot_ref[...], (((0,), (0,)), ((), ())), preferred_element_type=jnp.float32
        )
        for zh in range(group):
            for y in range(NYH):
                first = (zh * NYH + y) * rows
                piece = value[first : first + rows]
                if more:
                    piece = piece + refs[0][y, zh].astype(jnp.float32)
                refs[-1][y, zh] = piece.astype(jnp.bfloat16)

    return pl.pallas_call(
        kernel,
        grid_spec=pltpu.PrefetchScalarGridSpec(
            num_scalar_prefetch=1,
            grid=(NZH // group,),
            in_specs=[
                pl.BlockSpec((tokens, group * part), lambda n, core_ref: (0, core_ref[0] * (NZH // group) + n)),
                pl.BlockSpec((tokens, head), lambda n, core_ref: (0, NODE * part // head)),
            ]
            + [block] * len(more)
            + [pl.BlockSpec(memory_space=pl.ANY)] * len(after),
            out_specs=block,
        ),
        out_shape=pltpu.HBM(out, jnp.bfloat16) if more else jax.ShapeDtypeStruct(out, jnp.bfloat16),
        compiler_params=SMALL,
        cost_estimate=pl.CostEstimate(
            flops=tokens * NODE * part * head,
            bytes_accessed=tokens * width * 2,
            transcendentals=0,
        ),
    )(core, got, got, *more, *after)


def small_kernel(kernel, out, value, after=()):
    return pl.pallas_call(
        kernel,
        in_specs=[pl.BlockSpec(memory_space=pltpu.VMEM)] + [pl.BlockSpec(memory_space=pl.ANY)] * len(after),
        out_specs=pl.BlockSpec(memory_space=pltpu.VMEM),
        out_shape=jax.ShapeDtypeStruct(out, jnp.bfloat16),
        compiler_params=SMALL,
        cost_estimate=pl.CostEstimate(flops=value.size, bytes_accessed=value.size * 2, transcendentals=0),
    )(value, *after)


def total_of(ref, index):
    total = ref[(0,) + index].astype(jnp.float32)
    for i in range(1, ref.shape[0]):
        total = total + ref[(i,) + index].astype(jnp.float32)
    return total.astype(jnp.bfloat16)


PIECE, LANES = 16, 128


def pieces(rows, head):
    whole = (rows // PIECE) * (head // LANES)
    each = -(-whole // NZL)
    return each, [
        (p // each, p % each * PIECE, p % (rows // PIECE) * PIECE, p // (rows // PIECE) * LANES) for p in range(whole)
    ]


def sum_y(value, after):
    ny, nzh, rows, head = value.shape
    each, where = pieces(rows, head)

    def kernel(value_ref, *refs):
        out_ref = refs[-1]
        for zh in range(nzh):
            out_ref[zh, NZL - 1] = jnp.zeros(out_ref.shape[2:], jnp.bfloat16)
            for zl, slot, row, column in where:
                out_ref[zh, zl, slot : slot + PIECE] = total_of(
                    value_ref, (zh, slice(row, row + PIECE), slice(column, column + LANES))
                )

    return small_kernel(kernel, (nzh, NZL, each * PIECE, LANES), value, after)


def sum_z(value):
    def kernel(value_ref, out_ref):
        total = total_of(value_ref, ())
        for i in range(NYH * NZL):
            out_ref[i] = total

    return small_kernel(kernel, (NYH * NZL,) + value.shape[1:], value)


def join(value, rows, head):
    _, where = pieces(rows, head)

    def kernel(value_ref, out_ref):
        for y in range(NYH):
            for zl, slot, row, column in where:
                piece = value_ref[y, zl, slot : slot + PIECE]
                for s in range(NEAR):
                    out_ref[s, y, row : row + PIECE, column : column + LANES] = piece

    return small_kernel(kernel, (NEAR, NYH, rows, head), value)


def input_gradient(peers, w_values, w_scales):
    head = w_values.shape[1]
    blocks = w_values.shape[0] // 128
    weight = (
        (w_values.astype(jnp.float32).reshape(blocks, 128, head) * w_scales[:, None, None])
        .reshape(blocks * 128, head)
        .astype(jnp.bfloat16)
    )
    columns = lax.dot_general(
        peers, weight, (((1,), (1,)), ((), ())), preferred_element_type=jnp.float32
    )
    return columns.astype(jnp.bfloat16)


def gather_zh(cotangent):
    return [cotangent] + [
        lax.ppermute(cotangent, "zh", [(i, (i + k) % NZH) for i in range(NZH)]) for k in range(1, NZH)
    ]


def gather_node(mine):
    here = lax.axis_index("zh")
    stack = jnp.stack(mine)
    ordered = jnp.concatenate(
        [lax.dynamic_slice_in_dim(stack, (here - j) % NZH, 1, 0) for j in range(NZH)], axis=0
    )
    other = lax.ppermute(ordered, "c", [(0, 1), (1, 0)])
    first = lax.axis_index("c") == 0
    return jnp.stack([jnp.where(first, ordered, other), jnp.where(first, other, ordered)], axis=1)


def local(acts, cotangent, w_values, w_scales):
    tok, width = acts.shape
    head = cotangent.shape[1]
    owned = width // NODE
    part = owned // NEAR
    rows = part // NYH
    factor = (tok * NYH * NYL * NX * NZL * NZH * NC) ** (-0.5)

    core = lax.axis_index("c")[None]
    got = exchange(lay_out(acts, cotangent), ("x", "yl")).reshape(NEAR * tok, NODE * part + head)
    mine = gather_zh(cotangent)
    theirs = product(got, head, 1 - core, after=mine[1:])
    chip = product(got, head, core, received=lax.ppermute(theirs, "c", [(0, 1), (1, 0)]))

    over_y = exchange(chip, "yh")
    peers = gather_node(mine).reshape(NODE * tok, head)
    input_grad = input_gradient(peers, w_values, w_scales)

    slots = sum_y(over_y, [input_grad])
    slots = slots.reshape((NZH * NZL,) + slots.shape[2:])
    copies = sum_z(exchange(slots, ("zh", "zl")))
    back = exchange(copies, ("yh", "zl"))
    back = join(back.reshape((NYH, NZL) + back.shape[1:]), rows, head)
    full = exchange(back, ("x", "yl")).reshape(owned, head)
    return (input_grad, full.astype(jnp.float32) * factor)


def solution(mesh):
    fine = Mesh(mesh.devices.reshape(SIZES), AXES)
    dp, node = ("yh", "yl", "x", "zl"), ("zh", "c")
    placed = (P(dp + node, None), P(dp + node, None), P(node, None), P(node))
    return jax.shard_map(
        local,
        mesh=fine,
        in_specs=placed,
        out_specs=(P(dp, node), P(node, None)),
        check_vma=False,
    )
```

```python
import jax
import jax.numpy as jnp
from jax import lax
from jax.experimental import pallas as pl
from jax.experimental.pallas import tpu as pltpu
from jax.sharding import Mesh
from jax.sharding import PartitionSpec as P

AXES = ("yh", "yl", "x", "zl", "zh", "c")
NYH, NYL, NX, NZL, NZH, NC = SIZES = (4, 2, 4, 3, 4, 2)
NODE = NZH * NC
NEAR = NX * NYL
LARGE = pltpu.CompilerParams(vmem_limit_bytes=60 * 2**20)
SMALL = pltpu.CompilerParams(vmem_limit_bytes=12 * 2**20)


def exchange(value, axes):
    return lax.all_to_all(value, axes, split_axis=0, concat_axis=0, tiled=True)


def lay_out(acts, cotangent):
    tok, width = acts.shape
    head = cotangent.shape[1]
    part = width // (NODE * NEAR)
    step = 32

    def kernel(acts_ref, cot_ref, out_ref):
        for s in range(NEAR):
            for c in range(NC):
                for zh in range(NZH):
                    to, source = (c * NZH + zh) * part, ((zh * NC + c) * NEAR + s) * part
                    out_ref[s, :, to : to + part] = acts_ref[:, source : source + part]
            out_ref[s, :, NODE * part :] = cot_ref[...]

    out = (NEAR, tok, NODE * part + head)
    return pl.pallas_call(
        kernel,
        grid=(tok // step,),
        in_specs=[
            pl.BlockSpec((step, width), lambda i: (i, 0)),
            pl.BlockSpec((step, head), lambda i: (i, 0)),
        ],
        out_specs=pl.BlockSpec((NEAR, step, out[2]), lambda i: (0, i, 0)),
        out_shape=pltpu.HBM(out, jnp.bfloat16),
        compiler_params=LARGE,
        cost_estimate=pl.CostEstimate(flops=0, bytes_accessed=4 * NEAR * tok * out[2], transcendentals=0),
    )(acts, cotangent)


def product(got, head, core, received=None, after=()):
    tokens, width = got.shape
    part = (width - head) // NODE
    rows = part // NYH
    group = 2
    out = (NYH, NZH, rows, head)
    block = pl.BlockSpec((NYH, group, rows, head), lambda n, core_ref: (0, n, 0, 0))
    more = [] if received is None else [received]

    def kernel(core_ref, acts_ref, cot_ref, *refs):
        value = lax.dot_general(
            acts_ref[...], cot_ref[...], (((0,), (0,)), ((), ())), preferred_element_type=jnp.float32
        )
        for zh in range(group):
            for y in range(NYH):
                first = (zh * NYH + y) * rows
                piece = value[first : first + rows]
                if more:
                    piece = piece + refs[0][y, zh].astype(jnp.float32)
                refs[-1][y, zh] = piece.astype(jnp.bfloat16)

    return pl.pallas_call(
        kernel,
        grid_spec=pltpu.PrefetchScalarGridSpec(
            num_scalar_prefetch=1,
            grid=(NZH // group,),
            in_specs=[
                pl.BlockSpec((tokens, group * part), lambda n, core_ref: (0, core_ref[0] * (NZH // group) + n)),
                pl.BlockSpec((tokens, head), lambda n, core_ref: (0, NODE * part // head)),
            ]
            + [block] * len(more)
            + [pl.BlockSpec(memory_space=pl.ANY)] * len(after),
            out_specs=block,
        ),
        out_shape=pltpu.HBM(out, jnp.bfloat16) if more else jax.ShapeDtypeStruct(out, jnp.bfloat16),
        compiler_params=SMALL,
        cost_estimate=pl.CostEstimate(
            flops=tokens * NODE * part * head,
            bytes_accessed=tokens * width * 2,
            transcendentals=0,
        ),
    )(core, got, got, *more, *after)


def small_kernel(kernel, out, value, after=()):
    return pl.pallas_call(
        kernel,
        in_specs=[pl.BlockSpec(memory_space=pltpu.VMEM)] + [pl.BlockSpec(memory_space=pl.ANY)] * len(after),
        out_specs=pl.BlockSpec(memory_space=pltpu.VMEM),
        out_shape=jax.ShapeDtypeStruct(out, jnp.bfloat16),
        compiler_params=SMALL,
        cost_estimate=pl.CostEstimate(flops=value.size, bytes_accessed=value.size * 2, transcendentals=0),
    )(value, *after)


def total_of(ref, index):
    total = ref[(0,) + index].astype(jnp.float32)
    for i in range(1, ref.shape[0]):
        total = total + ref[(i,) + index].astype(jnp.float32)
    return total.astype(jnp.bfloat16)


PIECE, LANES = 16, 128


def pieces(rows, head):
    whole = (rows // PIECE) * (head // LANES)
    each = -(-whole // NZL)
    return each, [
        (p // each, p % each * PIECE, p % (rows // PIECE) * PIECE, p // (rows // PIECE) * LANES) for p in range(whole)
    ]


def sum_y(value, after):
    ny, nzh, rows, head = value.shape
    each, where = pieces(rows, head)

    def kernel(value_ref, *refs):
        out_ref = refs[-1]
        for zh in range(nzh):
            out_ref[zh, NZL - 1] = jnp.zeros(out_ref.shape[2:], jnp.bfloat16)
            for zl, slot, row, column in where:
                out_ref[zh, zl, slot : slot + PIECE] = total_of(
                    value_ref, (zh, slice(row, row + PIECE), slice(column, column + LANES))
                )

    return small_kernel(kernel, (nzh, NZL, each * PIECE, LANES), value, after)


def sum_z(value):
    def kernel(value_ref, out_ref):
        total = total_of(value_ref, ())
        for i in range(NYH * NZL):
            out_ref[i] = total

    return small_kernel(kernel, (NYH * NZL,) + value.shape[1:], value)


def join(value, rows, head):
    _, where = pieces(rows, head)

    def kernel(value_ref, out_ref):
        for y in range(NYH):
            for zl, slot, row, column in where:
                piece = value_ref[y, zl, slot : slot + PIECE]
                for s in range(NEAR):
                    out_ref[s, y, row : row + PIECE, column : column + LANES] = piece

    return small_kernel(kernel, (NEAR, NYH, rows, head), value)


def input_gradient(peers, w_values, w_scales):
    head = w_values.shape[1]
    blocks = w_values.shape[0] // 128
    weight = (
        (w_values.astype(jnp.float32).reshape(blocks, 128, head) * w_scales[:, None, None])
        .reshape(blocks * 128, head)
        .astype(jnp.bfloat16)
    )
    columns = lax.dot_general(
        peers, weight, (((1,), (1,)), ((), ())), preferred_element_type=jnp.float32
    )
    return columns.astype(jnp.bfloat16)


def gather_zh(cotangent):
    return [cotangent] + [
        lax.ppermute(cotangent, "zh", [(i, (i + k) % NZH) for i in range(NZH)]) for k in range(1, NZH)
    ]


def in_order(mine):
    def kernel(zh_ref, *refs):
        for k in range(NZH):
            refs[-1][lax.rem(zh_ref[0] + (NZH - k), NZH)] = refs[k][...]

    return pl.pallas_call(
        kernel,
        in_specs=[pl.BlockSpec(memory_space=pltpu.SMEM)] + [pl.BlockSpec(memory_space=pltpu.VMEM)] * NZH,
        out_specs=pl.BlockSpec(memory_space=pltpu.VMEM),
        out_shape=jax.ShapeDtypeStruct((NZH,) + mine[0].shape, jnp.bfloat16),
        compiler_params=SMALL,
        cost_estimate=pl.CostEstimate(flops=0, bytes_accessed=4 * NZH * mine[0].size, transcendentals=0),
    )(lax.axis_index("zh")[None], *mine)


def gather_node(ordered):
    other = lax.ppermute(ordered, "c", [(0, 1), (1, 0)])
    first = lax.axis_index("c") == 0
    return jnp.stack([jnp.where(first, ordered, other), jnp.where(first, other, ordered)], axis=1)


def local(acts, cotangent, w_values, w_scales):
    tok, width = acts.shape
    head = cotangent.shape[1]
    owned = width // NODE
    part = owned // NEAR
    rows = part // NYH
    factor = (tok * NYH * NYL * NX * NZL * NZH * NC) ** (-0.5)

    core = lax.axis_index("c")[None]
    got = exchange(lay_out(acts, cotangent), ("x", "yl")).reshape(NEAR * tok, NODE * part + head)
    ordered = in_order(gather_zh(cotangent))
    theirs = product(got, head, 1 - core, after=[ordered])
    chip = product(got, head, core, received=lax.ppermute(theirs, "c", [(0, 1), (1, 0)]))

    over_y = exchange(chip, "yh")
    peers = gather_node(ordered).reshape(NODE * tok, head)
    input_grad = input_gradient(peers, w_values, w_scales)

    slots = sum_y(over_y, [input_grad])
    slots = slots.reshape((NZH * NZL,) + slots.shape[2:])
    copies = sum_z(exchange(slots, ("zh", "zl")))
    back = exchange(copies, ("yh", "zl"))
    back = join(back.reshape((NYH, NZL) + back.shape[1:]), rows, head)
    full = exchange(back, ("x", "yl")).reshape(owned, head)
    return (input_grad, full.astype(jnp.float32) * factor)


def solution(mesh):
    fine = Mesh(mesh.devices.reshape(SIZES), AXES)
    dp, node = ("yh", "yl", "x", "zl"), ("zh", "c")
    placed = (P(dp + node, None), P(dp + node, None), P(node, None), P(node))
    return jax.shard_map(
        local,
        mesh=fine,
        in_specs=placed,
        out_specs=(P(dp, node), P(node, None)),
        check_vma=False,
    )
```

```python
import jax
import jax.numpy as jnp
from jax import lax
from jax.experimental import pallas as pl
from jax.experimental.pallas import tpu as pltpu
from jax.sharding import Mesh
from jax.sharding import PartitionSpec as P

AXES = ("yh", "yl", "x", "zl", "zh", "c")
NYH, NYL, NX, NZL, NZH, NC = SIZES = (4, 2, 4, 3, 4, 2)
NODE = NZH * NC
NEAR = NX * NYL
LARGE = pltpu.CompilerParams(vmem_limit_bytes=60 * 2**20)
SMALL = pltpu.CompilerParams(vmem_limit_bytes=12 * 2**20)


def exchange(value, axes):
    return lax.all_to_all(value, axes, split_axis=0, concat_axis=0, tiled=True)


def lay_out(acts, cotangent):
    tok, width = acts.shape
    head = cotangent.shape[1]
    part = width // (NODE * NEAR)
    step = 16
    chunks = tok // step
    out = (NEAR, tok, NODE * part + head)

    def kernel(acts_ref, cot_ref, out_ref, acts_in, cot_in, laid, acts_sem, cot_sem, out_sem):
        def rows(i):
            return pl.ds(i * step, step)

        cot_copy = pltpu.make_async_copy(cot_ref, cot_in, cot_sem)
        cot_copy.start()
        reads = [
            pltpu.make_async_copy(acts_ref.at[rows(i)], acts_in.at[rows(i)], acts_sem.at[i]) for i in range(chunks)
        ]
        for read in reads:
            read.start()
        cot_copy.wait()
        writes = []
        for i in range(chunks):
            reads[i].wait()
            for s in range(NEAR):
                for c in range(NC):
                    for zh in range(NZH):
                        to, source = (c * NZH + zh) * part, ((zh * NC + c) * NEAR + s) * part
                        laid[s, rows(i), to : to + part] = acts_in[rows(i), source : source + part]
                laid[s, rows(i), NODE * part :] = cot_in[rows(i), :]
            writes.append(pltpu.make_async_copy(laid.at[:, rows(i)], out_ref.at[:, rows(i)], out_sem.at[i]))
            writes[-1].start()
        for write in writes:
            write.wait()

    return pl.pallas_call(
        kernel,
        in_specs=[pl.BlockSpec(memory_space=pl.ANY)] * 2,
        out_specs=pl.BlockSpec(memory_space=pl.ANY),
        out_shape=pltpu.HBM(out, jnp.bfloat16),
        scratch_shapes=[
            pltpu.VMEM((tok, width), jnp.bfloat16),
            pltpu.VMEM((tok, head), jnp.bfloat16),
            pltpu.VMEM(out, jnp.bfloat16),
            pltpu.SemaphoreType.DMA((chunks,)),
            pltpu.SemaphoreType.DMA,
            pltpu.SemaphoreType.DMA((chunks,)),
        ],
        compiler_params=LARGE,
        cost_estimate=pl.CostEstimate(flops=0, bytes_accessed=4 * NEAR * tok * out[2], transcendentals=0),
    )(acts, cotangent)


def product(got, head, core, received=None, after=()):
    tokens, width = got.shape
    part = (width - head) // NODE
    rows = part // NYH
    group = 2
    out = (NYH, NZH, rows, head)
    block = pl.BlockSpec((NYH, group, rows, head), lambda n, core_ref: (0, n, 0, 0))
    more = [] if received is None else [received]

    def kernel(core_ref, acts_ref, cot_ref, *refs):
        value = lax.dot_general(
            acts_ref[...], cot_ref[...], (((0,), (0,)), ((), ())), preferred_element_type=jnp.float32
        )
        for zh in range(group):
            for y in range(NYH):
                first = (zh * NYH + y) * rows
                piece = value[first : first + rows]
                if more:
                    piece = piece + refs[0][y, zh].astype(jnp.float32)
                refs[-1][y, zh] = piece.astype(jnp.bfloat16)

    return pl.pallas_call(
        kernel,
        grid_spec=pltpu.PrefetchScalarGridSpec(
            num_scalar_prefetch=1,
            grid=(NZH // group,),
            in_specs=[
                pl.BlockSpec((tokens, group * part), lambda n, core_ref: (0, core_ref[0] * (NZH // group) + n)),
                pl.BlockSpec((tokens, head), lambda n, core_ref: (0, NODE * part // head)),
            ]
            + [block] * len(more)
            + [pl.BlockSpec(memory_space=pl.ANY)] * len(after),
            out_specs=block,
        ),
        out_shape=pltpu.HBM(out, jnp.bfloat16) if more else jax.ShapeDtypeStruct(out, jnp.bfloat16),
        compiler_params=SMALL,
        cost_estimate=pl.CostEstimate(
            flops=tokens * NODE * part * head,
            bytes_accessed=tokens * width * 2,
            transcendentals=0,
        ),
    )(core, got, got, *more, *after)


def small_kernel(kernel, out, value, after=()):
    return pl.pallas_call(
        kernel,
        in_specs=[pl.BlockSpec(memory_space=pltpu.VMEM)] + [pl.BlockSpec(memory_space=pl.ANY)] * len(after),
        out_specs=pl.BlockSpec(memory_space=pltpu.VMEM),
        out_shape=jax.ShapeDtypeStruct(out, jnp.bfloat16),
        compiler_params=SMALL,
        cost_estimate=pl.CostEstimate(flops=value.size, bytes_accessed=value.size * 2, transcendentals=0),
    )(value, *after)


def total_of(ref, index):
    total = ref[(0,) + index].astype(jnp.float32)
    for i in range(1, ref.shape[0]):
        total = total + ref[(i,) + index].astype(jnp.float32)
    return total.astype(jnp.bfloat16)


PIECE, LANES = 16, 128


def pieces(rows, head):
    whole = (rows // PIECE) * (head // LANES)
    each = -(-whole // NZL)
    return each, [
        (p // each, p % each * PIECE, p % (rows // PIECE) * PIECE, p // (rows // PIECE) * LANES) for p in range(whole)
    ]


def sum_y(value, after):
    ny, nzh, rows, head = value.shape
    each, where = pieces(rows, head)

    def kernel(value_ref, *refs):
        out_ref = refs[-1]
        for zh in range(nzh):
            out_ref[zh, NZL - 1] = jnp.zeros(out_ref.shape[2:], jnp.bfloat16)
            for zl, slot, row, column in where:
                out_ref[zh, zl, slot : slot + PIECE] = total_of(
                    value_ref, (zh, slice(row, row + PIECE), slice(column, column + LANES))
                )

    return small_kernel(kernel, (nzh, NZL, each * PIECE, LANES), value, after)


def sum_z(value):
    def kernel(value_ref, out_ref):
        total = total_of(value_ref, ())
        for i in range(NYH * NZL):
            out_ref[i] = total

    return small_kernel(kernel, (NYH * NZL,) + value.shape[1:], value)


def join(value, rows, head):
    _, where = pieces(rows, head)

    def kernel(value_ref, out_ref):
        for y in range(NYH):
            for zl, slot, row, column in where:
                piece = value_ref[y, zl, slot : slot + PIECE]
                for s in range(NEAR):
                    out_ref[s, y, row : row + PIECE, column : column + LANES] = piece

    return small_kernel(kernel, (NEAR, NYH, rows, head), value)


def input_gradient(peers, w_values, w_scales):
    head = w_values.shape[1]
    blocks = w_values.shape[0] // 128
    weight = (
        (w_values.astype(jnp.float32).reshape(blocks, 128, head) * w_scales[:, None, None])
        .reshape(blocks * 128, head)
        .astype(jnp.bfloat16)
    )
    columns = lax.dot_general(
        peers, weight, (((1,), (1,)), ((), ())), preferred_element_type=jnp.float32
    )
    return columns.astype(jnp.bfloat16)


def gather_zh(cotangent):
    return [cotangent] + [
        lax.ppermute(cotangent, "zh", [(i, (i + k) % NZH) for i in range(NZH)]) for k in range(1, NZH)
    ]


def in_order(mine):
    def kernel(zh_ref, *refs):
        for k in range(NZH):
            refs[-1][lax.rem(zh_ref[0] + (NZH - k), NZH)] = refs[k][...]

    return pl.pallas_call(
        kernel,
        in_specs=[pl.BlockSpec(memory_space=pltpu.SMEM)] + [pl.BlockSpec(memory_space=pltpu.VMEM)] * NZH,
        out_specs=pl.BlockSpec(memory_space=pltpu.VMEM),
        out_shape=jax.ShapeDtypeStruct((NZH,) + mine[0].shape, jnp.bfloat16),
        compiler_params=SMALL,
        cost_estimate=pl.CostEstimate(flops=0, bytes_accessed=4 * NZH * mine[0].size, transcendentals=0),
    )(lax.axis_index("zh")[None], *mine)


def gather_node(ordered):
    other = lax.ppermute(ordered, "c", [(0, 1), (1, 0)])
    first = lax.axis_index("c") == 0
    return jnp.stack([jnp.where(first, ordered, other), jnp.where(first, other, ordered)], axis=1)


def local(acts, cotangent, w_values, w_scales):
    tok, width = acts.shape
    head = cotangent.shape[1]
    owned = width // NODE
    part = owned // NEAR
    rows = part // NYH
    factor = (tok * NYH * NYL * NX * NZL * NZH * NC) ** (-0.5)

    core = lax.axis_index("c")[None]
    got = exchange(lay_out(acts, cotangent), ("yl", "x")).reshape(NEAR * tok, NODE * part + head)
    ordered = in_order(gather_zh(cotangent))
    theirs = product(got, head, 1 - core, after=[ordered])
    chip = product(got, head, core, received=lax.ppermute(theirs, "c", [(0, 1), (1, 0)]))

    over_y = exchange(chip, "yh")
    peers = gather_node(ordered).reshape(NODE * tok, head)
    input_grad = input_gradient(peers, w_values, w_scales)

    slots = sum_y(over_y, [input_grad])
    slots = slots.reshape((NZH * NZL,) + slots.shape[2:])
    copies = sum_z(exchange(slots, ("zh", "zl")))
    back = exchange(copies, ("yh", "zl"))
    back = join(back.reshape((NYH, NZL) + back.shape[1:]), rows, head)
    full = exchange(back, ("yl", "x")).reshape(owned, head)
    return (input_grad, full.astype(jnp.float32) * factor)


def solution(mesh):
    fine = Mesh(mesh.devices.reshape(SIZES), AXES)
    dp, node = ("yh", "yl", "x", "zl"), ("zh", "c")
    placed = (P(dp + node, None), P(dp + node, None), P(node, None), P(node))
    return jax.shard_map(
        local,
        mesh=fine,
        in_specs=placed,
        out_specs=(P(dp, node), P(node, None)),
        check_vma=False,
    )
```

```python
import jax
import jax.numpy as jnp
from jax import lax
from jax.experimental import pallas as pl
from jax.experimental.pallas import tpu as pltpu
from jax.sharding import Mesh
from jax.sharding import PartitionSpec as P

AXES = ("yh", "yl", "x", "zl", "zh", "c")
NYH, NYL, NX, NZL, NZH, NC = SIZES = (4, 2, 4, 3, 4, 2)
NODE = NZH * NC
NEAR = NX * NYL
LARGE = pltpu.CompilerParams(vmem_limit_bytes=60 * 2**20)
SMALL = pltpu.CompilerParams(vmem_limit_bytes=12 * 2**20)


def exchange(value, axes, groups=None):
    return lax.all_to_all(value, axes, split_axis=0, concat_axis=0, axis_index_groups=groups, tiled=True)


def exchange_near(value):
    groups = [
        [(((yh + (core and yl == 0)) % NYH * NYL + yl) * NX + x) * NC + core for yl in range(NYL) for x in range(NX)]
        for core in range(NC)
        for yh in range(NYH)
    ]
    return exchange(value, ("yh", "yl", "x", "c"), groups)


def lay_out(acts, cotangent):
    tok, width = acts.shape
    head = cotangent.shape[1]
    part = width // (NODE * NEAR)
    step = 16
    chunks = tok // step
    out = (NEAR, tok, NODE * part + head)

    def kernel(acts_ref, cot_ref, out_ref, acts_in, cot_in, laid, acts_sem, cot_sem, out_sem):
        def rows(i):
            return pl.ds(i * step, step)

        cot_copy = pltpu.make_async_copy(cot_ref, cot_in, cot_sem)
        cot_copy.start()
        reads = [
            pltpu.make_async_copy(acts_ref.at[rows(i)], acts_in.at[rows(i)], acts_sem.at[i]) for i in range(chunks)
        ]
        for read in reads:
            read.start()
        cot_copy.wait()
        writes = []
        for i in range(chunks):
            reads[i].wait()
            for s in range(NEAR):
                for c in range(NC):
                    for zh in range(NZH):
                        to, source = (c * NZH + zh) * part, ((zh * NC + c) * NEAR + s) * part
                        laid[s, rows(i), to : to + part] = acts_in[rows(i), source : source + part]
                laid[s, rows(i), NODE * part :] = cot_in[rows(i), :]
            writes.append(pltpu.make_async_copy(laid.at[:, rows(i)], out_ref.at[:, rows(i)], out_sem.at[i]))
            writes[-1].start()
        for write in writes:
            write.wait()

    return pl.pallas_call(
        kernel,
        in_specs=[pl.BlockSpec(memory_space=pl.ANY)] * 2,
        out_specs=pl.BlockSpec(memory_space=pl.ANY),
        out_shape=pltpu.HBM(out, jnp.bfloat16),
        scratch_shapes=[
            pltpu.VMEM((tok, width), jnp.bfloat16),
            pltpu.VMEM((tok, head), jnp.bfloat16),
            pltpu.VMEM(out, jnp.bfloat16),
            pltpu.SemaphoreType.DMA((chunks,)),
            pltpu.SemaphoreType.DMA,
            pltpu.SemaphoreType.DMA((chunks,)),
        ],
        compiler_params=LARGE,
        cost_estimate=pl.CostEstimate(flops=0, bytes_accessed=4 * NEAR * tok * out[2], transcendentals=0),
    )(acts, cotangent)


def product(got, head, core, received=None, after=()):
    tokens, width = got.shape
    part = (width - head) // NODE
    rows = part // NYH
    group = 2
    out = (NYH, NZH, rows, head)
    block = pl.BlockSpec((NYH, group, rows, head), lambda n, core_ref: (0, n, 0, 0))
    more = [] if received is None else [received]

    def kernel(core_ref, acts_ref, cot_ref, *refs):
        value = lax.dot_general(
            acts_ref[...], cot_ref[...], (((0,), (0,)), ((), ())), preferred_element_type=jnp.float32
        )
        for zh in range(group):
            for y in range(NYH):
                first = (zh * NYH + y) * rows
                piece = value[first : first + rows]
                if more:
                    piece = piece + refs[0][y, zh].astype(jnp.float32)
                refs[-1][y, zh] = piece.astype(jnp.bfloat16)

    return pl.pallas_call(
        kernel,
        grid_spec=pltpu.PrefetchScalarGridSpec(
            num_scalar_prefetch=1,
            grid=(NZH // group,),
            in_specs=[
                pl.BlockSpec((tokens, group * part), lambda n, core_ref: (0, core_ref[0] * (NZH // group) + n)),
                pl.BlockSpec((tokens, head), lambda n, core_ref: (0, NODE * part // head)),
            ]
            + [block] * len(more)
            + [pl.BlockSpec(memory_space=pl.ANY)] * len(after),
            out_specs=block,
        ),
        out_shape=pltpu.HBM(out, jnp.bfloat16) if more else jax.ShapeDtypeStruct(out, jnp.bfloat16),
        compiler_params=SMALL,
        cost_estimate=pl.CostEstimate(
            flops=tokens * NODE * part * head,
            bytes_accessed=tokens * width * 2,
            transcendentals=0,
        ),
    )(core, got, got, *more, *after)


def small_kernel(kernel, out, value, after=()):
    return pl.pallas_call(
        kernel,
        in_specs=[pl.BlockSpec(memory_space=pltpu.VMEM)] + [pl.BlockSpec(memory_space=pl.ANY)] * len(after),
        out_specs=pl.BlockSpec(memory_space=pltpu.VMEM),
        out_shape=jax.ShapeDtypeStruct(out, jnp.bfloat16),
        compiler_params=SMALL,
        cost_estimate=pl.CostEstimate(flops=value.size, bytes_accessed=value.size * 2, transcendentals=0),
    )(value, *after)


def total_of(ref, index):
    total = ref[(0,) + index].astype(jnp.float32)
    for i in range(1, ref.shape[0]):
        total = total + ref[(i,) + index].astype(jnp.float32)
    return total.astype(jnp.bfloat16)


PIECE, LANES = 16, 128


def pieces(rows, head):
    whole = (rows // PIECE) * (head // LANES)
    each = -(-whole // NZL)
    return each, [
        (p // each, p % each * PIECE, p % (rows // PIECE) * PIECE, p // (rows // PIECE) * LANES) for p in range(whole)
    ]


def sum_y(value, after):
    ny, nzh, rows, head = value.shape
    each, where = pieces(rows, head)

    def kernel(value_ref, *refs):
        out_ref = refs[-1]
        for zh in range(nzh):
            out_ref[zh, NZL - 1] = jnp.zeros(out_ref.shape[2:], jnp.bfloat16)
            for zl, slot, row, column in where:
                out_ref[zh, zl, slot : slot + PIECE] = total_of(
                    value_ref, (zh, slice(row, row + PIECE), slice(column, column + LANES))
                )

    return small_kernel(kernel, (nzh, NZL, each * PIECE, LANES), value, after)


def sum_z(value):
    def kernel(value_ref, out_ref):
        total = total_of(value_ref, ())
        for i in range(NYH * NZL):
            out_ref[i] = total

    return small_kernel(kernel, (NYH * NZL,) + value.shape[1:], value)


def join(value, rows, head):
    _, where = pieces(rows, head)

    def kernel(value_ref, out_ref):
        for y in range(NYH):
            for zl, slot, row, column in where:
                piece = value_ref[zl, y, slot : slot + PIECE]
                for s in range(NEAR):
                    out_ref[s, y, row : row + PIECE, column : column + LANES] = piece

    return small_kernel(kernel, (NEAR, NYH, rows, head), value)


def input_gradient(peers, w_values, w_scales):
    head = w_values.shape[1]
    blocks = w_values.shape[0] // 128
    weight = (
        (w_values.astype(jnp.float32).reshape(blocks, 128, head) * w_scales[:, None, None])
        .reshape(blocks * 128, head)
        .astype(jnp.bfloat16)
    )
    columns = lax.dot_general(
        peers, weight, (((1,), (1,)), ((), ())), preferred_element_type=jnp.float32
    )
    return columns.astype(jnp.bfloat16)


def gather_zh(cotangent):
    return [cotangent] + [
        lax.ppermute(cotangent, "zh", [(i, (i + k) % NZH) for i in range(NZH)]) for k in range(1, NZH)
    ]


def in_order(mine):
    def kernel(zh_ref, *refs):
        for k in range(NZH):
            refs[-1][lax.rem(zh_ref[0] + (NZH - k), NZH)] = refs[k][...]

    return pl.pallas_call(
        kernel,
        in_specs=[pl.BlockSpec(memory_space=pltpu.SMEM)] + [pl.BlockSpec(memory_space=pltpu.VMEM)] * NZH,
        out_specs=pl.BlockSpec(memory_space=pltpu.VMEM),
        out_shape=jax.ShapeDtypeStruct((NZH,) + mine[0].shape, jnp.bfloat16),
        compiler_params=SMALL,
        cost_estimate=pl.CostEstimate(flops=0, bytes_accessed=4 * NZH * mine[0].size, transcendentals=0),
    )(lax.axis_index("zh")[None], *mine)


def gather_node(ordered):
    other = lax.ppermute(ordered, "c", [(0, 1), (1, 0)])
    first = lax.axis_index("c") == 0
    return jnp.stack([jnp.where(first, ordered, other), jnp.where(first, other, ordered)], axis=1)


def local(acts, cotangent, w_values, w_scales):
    tok, width = acts.shape
    head = cotangent.shape[1]
    owned = width // NODE
    part = owned // NEAR
    rows = part // NYH
    factor = (tok * NYH * NYL * NX * NZL * NZH * NC) ** (-0.5)

    core = lax.axis_index("c")[None]
    got = exchange_near(lay_out(acts, cotangent)).reshape(NEAR * tok, NODE * part + head)
    ordered = in_order(gather_zh(cotangent))
    theirs = product(got, head, 1 - core, after=[ordered])
    chip = product(got, head, core, received=lax.ppermute(theirs, "c", [(0, 1), (1, 0)]))

    over_y = exchange(chip, "yh")
    peers = gather_node(ordered).reshape(NODE * tok, head)
    input_grad = input_gradient(peers, w_values, w_scales)

    slots = sum_y(over_y, [input_grad])
    slots = slots.reshape((NZH * NZL,) + slots.shape[2:])
    copies = sum_z(exchange(slots, ("zh", "zl")))
    back = exchange(copies, ("zl", "yh"))
    back = join(back.reshape((NZL, NYH) + back.shape[1:]), rows, head)
    full = exchange_near(back).reshape(owned, head)
    return (input_grad, full.astype(jnp.float32) * factor)


def solution(mesh):
    fine = Mesh(mesh.devices.reshape(SIZES), AXES)
    dp, node = ("yh", "yl", "x", "zl"), ("zh", "c")
    placed = (P(dp + node, None), P(dp + node, None), P(node, None), P(node))
    return jax.shard_map(
        local,
        mesh=fine,
        in_specs=placed,
        out_specs=(P(dp, node), P(node, None)),
        check_vma=False,
    )
```
